32 devices in a mesh: dp: 4 (over z), tx: 2 (over core), ty: 4 (over y, x).
Axes of the slice: x: 2, y: 2, z: 4, core: 2. Of those that a mesh axis runs over, the one named last changes fastest.
Arguments:
- tokens: bfloat16 [2048, 2048], P('dp', 'tx'), may hold values from -6 to 6
- query_weight: bfloat16 [2048, 4, 512], P(None, 'ty', 'tx'), may hold values from -0.25 to 0.25
- key_value_weight: bfloat16 [2048, 4, 128], P(None, 'ty'), may hold values from -0.125 to 0.125
- output_weight: bfloat16 [4, 512, 2048], P('ty', 'tx'), may hold values from -0.5 to 0.5
- cache: bfloat16 [4, 4, 2048, 128], P('dp', 'ty'), may hold values from -300 to 300
- lengths: int32 [4], replicated, may hold values from 0 to 8192, as said below
- offsets: int32 [4], replicated, may hold values from 0 to 2047
- slots: int32 [4], replicated, may hold values from 0 to 3, each once
Outputs:
- mixed: bfloat16 [2048, 2048], P('dp', ('tx', 'ty'))
- new_cache: bfloat16 [4, 4, 2048, 128], P('dp', 'ty')
The draws below stay inside these ranges and needn't reach their ends.
Inputs may be any that keep to these rules, and one draw needn't show every extreme that they name: `lengths`: some request has exactly 8192 cached positions. `slots`: every slot belongs to exactly one request.
All inputs are finite; a program needn't handle non-finite values.
Results may differ from the reference program's by a relative error of at most 0.012.
The reference program's roundings to bfloat16 on the way count: a program that leaves them out, or rounds other values in their place, can miss the bound.
Values may be sent and summed in bfloat16 or wider, within the bound.
A program may use at most 64 MiB of HBM per device.

```python
import math
import jax
import jax.numpy as jnp
from jax import lax

MODEL_WIDTH = 2048
QUERY_HEADS = 32
KEY_VALUE_HEADS = 4
HEAD_SIZE = 64
WINDOW_LENGTH = 2048
MAXLEN = 8192
FRESH_TOKENS = 512
QUERY_PER_KV = 8
REQUEST_COUNT = 4
TOKENS = 2048


def draw_cache(key, part):
    rotary_base = jnp.clip(jax.random.normal(key, (REQUEST_COUNT, KEY_VALUE_HEADS, WINDOW_LENGTH, 2 * HEAD_SIZE), jnp.float32), -6.0, 6.0)
    return rotary_base.astype(jnp.bfloat16)


def draw_lengths(key, part):
    first_random_key, second_random_key = jax.random.split(key)
    drawn = jax.random.randint(first_random_key, (REQUEST_COUNT,), 0, 1025)
    cubed = drawn * drawn // 1024 * drawn
    counts = cubed // (1048576 // MAXLEN)
    chosen = jax.random.randint(second_random_key, (), 0, REQUEST_COUNT)
    return jnp.where(jnp.arange(REQUEST_COUNT) == chosen, MAXLEN, counts).astype(jnp.int32)


def with_ends(array, own_key, least, high):
    dims = array.shape
    spot = [jax.random.randint(jax.random.fold_in(own_key, axis), (), 0, dims[axis]) for axis in range(len(dims))]
    array = array.at[tuple(spot)].set(least)
    longest = dims.index(max(dims))
    spot[longest] = (spot[longest] + 1) % dims[longest]
    return array.at[tuple(spot)].set(high)


def block_scale(rng, dims, shards, smallest, top_value):
    loudness = 1.0
    for dim, parts in shards:
        steps = jax.random.uniform(jax.random.fold_in(jax.random.fold_in(rng, 6), dim), (parts,), jnp.float32, smallest / len(shards), top_value / len(shards))
        loudness = loudness * jnp.repeat(jnp.exp(steps), dims[dim] // parts).reshape((-1,) + (1,) * (len(dims) - 1 - dim))
    return loudness


def centred(own_key, shape, deviation, bound, cuts=(), held_as=jnp.bfloat16):
    level = block_scale(own_key, shape, cuts, -0.22, 0.18) if cuts else 1.0
    values = jax.random.normal(own_key, shape, jnp.float32) * deviation * level
    return jnp.minimum(jnp.maximum(values, -bound), bound).astype(held_as)


def setup_inputs(seed: int = 0) -> dict:
    streams_of = jax.random.split(jax.random.key(seed), 9)
    return {
        "tokens": centred(streams_of[0], (TOKENS, MODEL_WIDTH), 1.0, 6.0, ((0, 4), (1, 2))),
        "query_weight": centred(streams_of[1], (MODEL_WIDTH, KEY_VALUE_HEADS, QUERY_PER_KV * HEAD_SIZE), (MODEL_WIDTH // 4) ** -0.5, 0.25, ((1, 4), (2, 2))),
        "key_value_weight": centred(streams_of[2], (MODEL_WIDTH, KEY_VALUE_HEADS, 2 * HEAD_SIZE), MODEL_WIDTH ** -0.5, 0.125, ((1, 4),)),
        "output_weight": centred(streams_of[3], (KEY_VALUE_HEADS, QUERY_PER_KV * HEAD_SIZE, MODEL_WIDTH), (QUERY_HEADS * HEAD_SIZE // 16) ** -0.5, 0.5, ((0, 4), (1, 2))),
        "cache": draw_cache(jax.random.fold_in(streams_of[8], 71), 0),
        "lengths": draw_lengths(jax.random.fold_in(streams_of[8], 71), 0),
        "offsets": with_ends(jax.random.randint(streams_of[6], (REQUEST_COUNT,), 0, WINDOW_LENGTH), jax.random.fold_in(streams_of[6], 1), 0, WINDOW_LENGTH - 1).astype(jnp.int32),
        "slots": jax.random.permutation(streams_of[7], REQUEST_COUNT).astype(jnp.int32),
    }


EPS = 1e-05

def apply_rotary(values, token_positions):
    width = values.shape[-1]
    half_width = width // 2
    freqs = jnp.exp(jnp.arange(half_width, dtype=jnp.float32) * (-2.0 * math.log(10000.0) / width))
    angles = token_positions.astype(jnp.float32)[:, None] * freqs[None, :]
    cosine = jnp.cos(angles)[:, None, :]
    sine = jnp.sin(angles)[:, None, :]
    leading = values[..., :half_width]
    trailing = values[..., half_width:]
    return jnp.concatenate([leading * cosine - trailing * sine, trailing * cosine + leading * sine], axis=-1)

def reference(tokens, query_weight, key_value_weight, output_weight, cache, lengths, offsets, slots):
    floats = tokens.astype(jnp.float32)
    normalized_input = (floats * lax.rsqrt(lax.optimization_barrier(jnp.mean(floats * floats, axis=1, keepdims=True)) + EPS)).astype(jnp.bfloat16)
    queries = jnp.dot(normalized_input, query_weight.reshape(MODEL_WIDTH, QUERY_HEADS * HEAD_SIZE), preferred_element_type=jnp.float32)
    rotation_pairs = jnp.dot(normalized_input, key_value_weight.reshape(MODEL_WIDTH, KEY_VALUE_HEADS * 2 * HEAD_SIZE), preferred_element_type=jnp.float32)
    queries = queries.reshape(REQUEST_COUNT, FRESH_TOKENS, QUERY_HEADS, HEAD_SIZE)
    rotation_pairs = rotation_pairs.reshape(REQUEST_COUNT, FRESH_TOKENS, KEY_VALUE_HEADS, 2 * HEAD_SIZE)
    factor = 1.0 / math.sqrt(HEAD_SIZE)

    def attend(inputs):
        query_rows, pair, length, offset, slot = inputs
        token_positions = length + jnp.arange(FRESH_TOKENS, dtype=jnp.int32)
        query_rotated = apply_rotary(query_rows, token_positions).astype(jnp.bfloat16).reshape(FRESH_TOKENS, KEY_VALUE_HEADS, QUERY_PER_KV, HEAD_SIZE)
        new_keys = apply_rotary(pair[:, :, :HEAD_SIZE], token_positions).astype(jnp.bfloat16)
        new_values = pair[:, :, HEAD_SIZE:].astype(jnp.bfloat16)
        stored = lax.dynamic_index_in_dim(cache, slot, 0, keepdims=False)
        cycle = jnp.arange(WINDOW_LENGTH, dtype=jnp.int32)
        held = length - 1 - jnp.mod(offset - 1 - cycle, WINDOW_LENGTH)
        cache_mask = (held[None, :] >= 0) & (held[None, :] > token_positions[:, None] - WINDOW_LENGTH)
        rows = jnp.arange(FRESH_TOKENS, dtype=jnp.int32)
        new_mask = rows[None, :] <= rows[:, None]
        mask = jnp.concatenate([cache_mask, new_mask], axis=1)
        keys = jnp.concatenate([stored[:, :, :HEAD_SIZE], jnp.transpose(new_keys, (1, 0, 2))], axis=1)
        values = jnp.concatenate([stored[:, :, HEAD_SIZE:], jnp.transpose(new_values, (1, 0, 2))], axis=1)
        scores = jnp.einsum('qgjd,gkd->gjqk', query_rotated.astype(jnp.float32), keys.astype(jnp.float32)) * factor
        scores = jnp.where(mask[None, None], scores, -jnp.inf)
        top = lax.optimization_barrier(jnp.max(scores, axis=-1, keepdims=True))
        powers = jnp.exp(scores - top)
        total = lax.optimization_barrier(jnp.sum(powers, axis=-1, keepdims=True))
        weights = powers.astype(jnp.bfloat16)
        summed = jnp.einsum('gjqk,gkd->qgjd', weights.astype(jnp.float32), values.astype(jnp.float32))
        attended = (summed / jnp.transpose(total, (2, 0, 1, 3))).astype(jnp.bfloat16)
        entry = jnp.concatenate([new_keys, new_values], axis=-1)
        return (attended.reshape(FRESH_TOKENS, QUERY_HEADS * HEAD_SIZE), entry)
    attended, entries = lax.map(attend, (queries, rotation_pairs, lengths, offsets, slots))
    mixed = jnp.dot(attended.reshape(TOKENS, QUERY_HEADS * HEAD_SIZE), output_weight.reshape(QUERY_HEADS * HEAD_SIZE, MODEL_WIDTH), preferred_element_type=jnp.float32).astype(jnp.bfloat16)
    cycle_rows = jnp.mod(offsets[:, None] + jnp.arange(FRESH_TOKENS, dtype=jnp.int32)[None, :], WINDOW_LENGTH)
    turned = jnp.transpose(cache, (0, 2, 1, 3))
    turned = turned.at[slots[:, None], cycle_rows].set(entries)
    new_cache = jnp.transpose(turned, (0, 2, 1, 3))
    return (mixed, new_cache)
```

```python
import functools
import math

import jax
import jax.numpy as jnp
from jax import lax
from jax.experimental import pallas as pl
from jax.experimental.pallas import tpu as pltpu
from jax.sharding import PartitionSpec as P

HEAD_SIZE = 64
WINDOW_LENGTH = 2048
EPS = 1e-05
LANES = 128
ROW_BLOCK = 128
PROJECT_ROWS = 256
KEY_CHUNK = 512
MESH = pl.DeviceIdType.MESH


def remote(src, dst, send_sem, recv_sem, device):
    return pltpu.make_async_remote_copy(
        src_ref=src, dst_ref=dst, send_sem=send_sem, recv_sem=recv_sem, device_id=device, device_id_type=MESH
    )


def contract_last(left, right):
    return lax.dot_general(left, right, (((1,), (1,)), ((), ())), preferred_element_type=jnp.float32)


def matmul(left, right):
    return jnp.dot(left, right, preferred_element_type=jnp.float32)


def kernel(
    zn, yn,
    tokens, query_weight, key_value_weight, output_weight, cache, cosine, sine, lengths, offsets, slots,
    mixed, new_cache,
    tok, qw, kvw, old, wbuf, spread, stage, kv, ents, qs, att, score, mine, psend, precv,
    local_sem, tok_sem, w_send, w_recv, s_send, s_recv, g_send, g_recv, half_sem, e_send, e_recv,
    a_send, a_recv, p_send, p_recv,
):
    me = lax.axis_index("dp")
    tx = lax.axis_index("tx")
    ty = lax.axis_index("ty")
    rows = tok.shape[1]
    half_width = tok.shape[2]
    cols = mixed.shape[1]
    heads = qs.shape[0]
    piece = spread.shape[1]
    half_rows = zn * piece
    blocks = rows // ROW_BLOCK
    sibling = {"tx": 1 - tx}

    def z_peer(d):
        return lax.rem(me + d, zn)

    def y_peer(d):
        return lax.rem(ty + d, yn)

    local = [
        pltpu.make_async_copy(tokens, tok.at[tx], local_sem.at[0]),
        pltpu.make_async_copy(query_weight, qw, local_sem.at[1]),
        pltpu.make_async_copy(key_value_weight, kvw, local_sem.at[2]),
        pltpu.make_async_copy(cache.at[0, 0], old, local_sem.at[3]),
        pltpu.make_async_copy(
            cache.at[0, 0, pl.ds(pl.multiple_of((tx * zn + me) * piece, piece), piece)],
            spread.at[0], local_sem.at[4],
        ),
    ]

    def w_columns(side, block):
        core = tx if side == 0 else 1 - tx
        return output_weight.at[0, :, pl.ds(pl.multiple_of((core * yn + block) * cols, cols), cols)]

    for side in range(2):
        local.append(pltpu.make_async_copy(w_columns(side, ty), wbuf.at[0, side], local_sem.at[5 + side]))
    for copy in local:
        copy.start()

    barrier = pltpu.get_barrier_semaphore()
    for d in range(1, zn):
        pl.semaphore_signal(barrier, inc=1, device_id={"dp": z_peer(d)}, device_id_type=MESH)
    for d in range(1, yn):
        pl.semaphore_signal(barrier, inc=1, device_id={"ty": y_peer(d)}, device_id_type=MESH)
    pl.semaphore_signal(barrier, inc=1, device_id=sibling, device_id_type=MESH)
    pl.semaphore_wait(barrier, zn + yn - 1)

    tok_copy = remote(tokens, tok.at[tx], tok_sem.at[0], tok_sem.at[1], sibling)
    tok_copy.start()
    spread_copies = []
    for d in range(1, zn):
        source = cache.at[0, 0, pl.ds(pl.multiple_of((tx * zn + z_peer(d)) * piece, piece), piece)]
        spread_copies.append(
            remote(source, spread.at[d], s_send.at[d], s_recv.at[d], {"dp": z_peer(d)})
        )
        spread_copies[-1].start()
    w_copies = []
    for d in range(1, yn):
        for side in range(2):
            w_copies.append(
                remote(
                    w_columns(side, y_peer(d)), wbuf.at[d, side], w_send.at[d, side], w_recv.at[d, side],
                    {"ty": y_peer(d)},
                )
            )
            w_copies[-1].start()

    length = lengths[me]
    offset = offsets[me]
    lane = lax.broadcasted_iota(jnp.int32, (PROJECT_ROWS, LANES), 1)
    first_half = lax.rem(lane, HEAD_SIZE) < HEAD_SIZE // 2
    key_lane = lane < HEAD_SIZE

    def project(step):
        at = pl.ds(step * PROJECT_ROWS, PROJECT_ROWS)
        left = tok[0, at, :].astype(jnp.float32)
        right = tok[1, at, :].astype(jnp.float32)
        squares = jnp.sum(left * left + right * right, axis=1, keepdims=True)
        scale = lax.rsqrt(squares * (1.0 / (2 * half_width)) + EPS)
        left = (left * scale).astype(jnp.bfloat16)
        right = (right * scale).astype(jnp.bfloat16)
        queries = matmul(left, qw[:half_width, :]) + matmul(right, qw[half_width:, :])
        pairs = matmul(left, kvw[:half_width, :]) + matmul(right, kvw[half_width:, :])
        cos = cosine[at, :]
        sin = sine[at, :]

        def rotary(u):
            turned = jnp.where(
                first_half,
                pltpu.roll(u, LANES - HEAD_SIZE // 2, 1),
                pltpu.roll(u, HEAD_SIZE // 2, 1),
            )
            return u * cos + turned * sin

        for pair in range(heads // 2):
            rot = rotary(queries[:, pair * LANES : (pair + 1) * LANES]).astype(jnp.bfloat16)
            rot = rot.astype(jnp.float32) * (1.0 / math.sqrt(HEAD_SIZE))
            even = jnp.where(key_lane, rot, 0.0)
            odd = jnp.where(key_lane, pltpu.roll(rot, HEAD_SIZE, 1), 0.0)
            qs[2 * pair, at, :] = even.astype(jnp.bfloat16)
            qs[2 * pair + 1, at, :] = odd.astype(jnp.bfloat16)
        entry = jnp.where(key_lane, rotary(pairs), pairs).astype(jnp.bfloat16)
        kv[pl.ds(WINDOW_LENGTH + step * PROJECT_ROWS, PROJECT_ROWS), :] = entry
        ents[0, at, :] = entry

    local[0].wait()
    local[1].wait()
    local[2].wait()
    tok_copy.wait_recv()
    project(0)

    local[4].wait()
    for copy in spread_copies:
        copy.wait_recv()
    own_rows = pl.ds(pl.multiple_of((tx * zn + me) * piece, piece), piece)
    gather_copies = []
    for e in range(zn):
        slot = slots[z_peer(e)]
        block = spread[lax.rem(me - slot + zn, zn)]
        if e == 0:
            kv[own_rows, :] = block
        else:
            stage[e] = block
            gather_copies.append(
                remote(stage.at[e], kv.at[own_rows], g_send.at[e], g_recv.at[e], {"dp": z_peer(e)})
            )
            gather_copies[-1].start()

    for step in range(1, rows // PROJECT_ROWS):
        project(step)

    for copy in gather_copies:
        copy.wait_recv()
    half = kv.at[pl.ds(pl.multiple_of(tx * half_rows, half_rows), half_rows)]
    half_copy = remote(half, half, half_sem.at[0], half_sem.at[1], sibling)
    half_copy.start()
    entry_copies = []
    for d in range(1, zn):
        entry_copies.append(
            remote(ents.at[0], ents.at[d], e_send.at[d], e_recv.at[d], {"dp": z_peer(d)})
        )
        entry_copies[-1].start()
    half_copy.wait_recv()

    stacked = heads * ROW_BLOCK
    chunks = kv.shape[0] // KEY_CHUNK
    old_chunks = WINDOW_LENGTH // KEY_CHUNK
    slices = KEY_CHUNK // LANES

    def att_copy(block, d):
        at = pl.ds(pl.multiple_of(block * ROW_BLOCK, ROW_BLOCK), ROW_BLOCK)
        return remote(
            att.at[0, at], att.at[d, at], a_send.at[block, d], a_recv.at[block, d], {"ty": y_peer(d)}
        )

    def attend(block, carry):
        start = pl.multiple_of(block * ROW_BLOCK, ROW_BLOCK)
        at = pl.ds(start, ROW_BLOCK)
        q = jnp.concatenate([qs[h, at, :] for h in range(heads)], axis=0)
        row = lax.rem(lax.broadcasted_iota(jnp.int32, (stacked, KEY_CHUNK), 0), ROW_BLOCK) + start
        column = lax.broadcasted_iota(jnp.int32, (1, KEY_CHUNK), 1)
        top = jnp.full((stacked, LANES), -jnp.inf, jnp.float32)
        for c in range(chunks):
            s = contract_last(q, kv[c * KEY_CHUNK : (c + 1) * KEY_CHUNK, :])
            if c < old_chunks:
                age = (offset - 1 - c * KEY_CHUNK - column) & (WINDOW_LENGTH - 1)
                last = jnp.where(age < length, WINDOW_LENGTH - 2 - age, -1)
                s = jnp.where(row <= last, s, -jnp.inf)
            else:
                s = jnp.where(row >= column + (c - old_chunks) * KEY_CHUNK, s, -jnp.inf)
            score[:, c * KEY_CHUNK : (c + 1) * KEY_CHUNK] = s
            for k in range(slices):
                top = jnp.maximum(top, s[:, k * LANES : (k + 1) * LANES])
        top = jnp.max(top, axis=1, keepdims=True)
        total = jnp.zeros((stacked, LANES), jnp.float32)
        summed = jnp.zeros((stacked, LANES), jnp.float32)
        for c in range(chunks):
            powers = jnp.exp(score[:, c * KEY_CHUNK : (c + 1) * KEY_CHUNK] - top)
            for k in range(slices):
                total = total + powers[:, k * LANES : (k + 1) * LANES]
            summed = summed + matmul(
                powers.astype(jnp.bfloat16), kv[c * KEY_CHUNK : (c + 1) * KEY_CHUNK, :]
            )
        result = summed / jnp.sum(total, axis=1, keepdims=True)
        low = lax.broadcasted_iota(jnp.int32, (ROW_BLOCK, LANES), 1) < HEAD_SIZE
        for pair in range(heads // 2):
            even = result[2 * pair * ROW_BLOCK : (2 * pair + 1) * ROW_BLOCK, :]
            odd = result[(2 * pair + 1) * ROW_BLOCK : (2 * pair + 2) * ROW_BLOCK, :]
            both = jnp.where(low, pltpu.roll(even, HEAD_SIZE, 1), odd)
            att[0, at, pair * LANES : (pair + 1) * LANES] = both.astype(jnp.bfloat16)
        for d in range(1, yn):
            att_copy(block, d).start()
        return carry

    lax.fori_loop(0, blocks, attend, 0)

    owner = jnp.int32(0)
    turn = jnp.int32(0)
    for r in range(zn):
        here = slots[r] == me
        owner = jnp.where(here, r, owner)
        turn = jnp.where(here, offsets[r], turn)
    for copy in entry_copies:
        copy.wait_recv()
    local[3].wait()
    entry = ents[lax.rem(me - owner + zn, zn)]
    target = lax.broadcasted_iota(jnp.int32, (KEY_CHUNK, rows), 1)
    for c in range(old_chunks):
        at = pl.ds(c * KEY_CHUNK, KEY_CHUNK)
        index = (lax.broadcasted_iota(jnp.int32, (KEY_CHUNK, rows), 0) + (c * KEY_CHUNK - turn)) & (
            WINDOW_LENGTH - 1
        )
        chosen = jnp.where(index == target, 1.0, 0.0).astype(jnp.bfloat16)
        written = matmul(chosen, entry)
        kept = old[at, :].astype(jnp.float32)
        new_cache[0, 0, at, :] = jnp.where(index[:, :LANES] < rows, written, kept).astype(jnp.bfloat16)

    for copy in w_copies:
        copy.wait_recv()
    local[5].wait()
    local[6].wait()
    part_copies = []
    for block in range(blocks):
        at = pl.ds(block * ROW_BLOCK, ROW_BLOCK)
        for d in range(1, yn):
            att_copy(block, d).wait_recv()
        pieces = [att[d, at, :] for d in range(yn)]
        other = matmul(pieces[0], wbuf[0, 1])
        for d in range(1, yn):
            other = other + matmul(pieces[d], wbuf[d, 1])
        psend[at, :] = other
        part_copies.append(
            remote(psend.at[at], precv.at[at], p_send.at[block], p_recv.at[block], sibling)
        )
        part_copies[-1].start()
        own = matmul(pieces[0], wbuf[0, 0])
        for d in range(1, yn):
            own = own + matmul(pieces[d], wbuf[d, 0])
        mine[at, :] = own
    for block in range(blocks):
        at = pl.ds(block * ROW_BLOCK, ROW_BLOCK)
        part_copies[block].wait_recv()
        mixed[at, :] = (mine[at, :] + precv[at, :]).astype(jnp.bfloat16)

    tok_copy.wait_send()
    half_copy.wait_send()
    for copy in spread_copies + w_copies + gather_copies + entry_copies + part_copies:
        copy.wait_send()
    for block in range(blocks):
        for d in range(1, yn):
            att_copy(block, d).wait_send()


def per_device(
    tokens, query_weight, key_value_weight, output_weight, cache, lengths, offsets, slots
):
    zn = lax.axis_size("dp")
    yn = lax.axis_size("ty")
    rows, half_width = tokens.shape
    width = 2 * half_width
    query_cols = query_weight.shape[2]
    heads = query_cols // HEAD_SIZE
    cols = width // (2 * yn)
    piece = WINDOW_LENGTH // (2 * zn)
    blocks = rows // ROW_BLOCK

    length = lengths[lax.axis_index("dp")]
    half_size = HEAD_SIZE // 2
    spot = jnp.arange(LANES, dtype=jnp.int32)
    freqs = jnp.exp(
        (spot % half_size).astype(jnp.float32) * (-2.0 * math.log(10000.0) / HEAD_SIZE)
    )
    positions = (length + jnp.arange(rows, dtype=jnp.int32)).astype(jnp.float32)
    angles = positions[:, None] * freqs[None, :]
    cosine = jnp.cos(angles)
    sine = jnp.where(spot[None, :] % HEAD_SIZE < half_size, -jnp.sin(angles), jnp.sin(angles))

    bf16 = jnp.bfloat16
    f32 = jnp.float32
    dma = pltpu.SemaphoreType.DMA
    anywhere = pl.BlockSpec(memory_space=pl.ANY)
    vmem = pl.BlockSpec(memory_space=pltpu.VMEM)
    smem = pl.BlockSpec(memory_space=pltpu.SMEM)
    flops = 2 * rows * (width * (query_cols + 2 * HEAD_SIZE + width // yn) + 4 * query_cols * (WINDOW_LENGTH + rows))
    return pl.pallas_call(
        functools.partial(kernel, zn, yn),
        out_shape=(
            jax.ShapeDtypeStruct((rows, cols), bf16),
            jax.ShapeDtypeStruct(cache.shape, bf16),
        ),
        in_specs=[anywhere] * 5 + [vmem] * 2 + [smem] * 3,
        out_specs=(vmem, vmem),
        scratch_shapes=[
            pltpu.VMEM((2, rows, half_width), bf16),
            pltpu.VMEM((width, query_cols), bf16),
            pltpu.VMEM((width, 2 * HEAD_SIZE), bf16),
            pltpu.VMEM((WINDOW_LENGTH, 2 * HEAD_SIZE), bf16),
            pltpu.VMEM((yn, 2, query_cols, cols), bf16),
            pltpu.VMEM((zn, piece, 2 * HEAD_SIZE), bf16),
            pltpu.VMEM((zn, piece, 2 * HEAD_SIZE), bf16),
            pltpu.VMEM((WINDOW_LENGTH + rows, 2 * HEAD_SIZE), bf16),
            pltpu.VMEM((zn, rows, 2 * HEAD_SIZE), bf16),
            pltpu.VMEM((heads, rows, LANES), bf16),
            pltpu.VMEM((yn, rows, query_cols), bf16),
            pltpu.VMEM((heads * ROW_BLOCK, WINDOW_LENGTH + rows), f32),
            pltpu.VMEM((rows, cols), f32),
            pltpu.VMEM((rows, cols), f32),
            pltpu.VMEM((rows, cols), f32),
            dma((7,)),
            dma((2,)),
            dma((yn, 2)),
            dma((yn, 2)),
            dma((zn,)),
            dma((zn,)),
            dma((zn,)),
            dma((zn,)),
            dma((2,)),
            dma((zn,)),
            dma((zn,)),
            dma((blocks, yn)),
            dma((blocks, yn)),
            dma((blocks,)),
            dma((blocks,)),
        ],
        compiler_params=pltpu.CompilerParams(
            collective_id=0, has_side_effects=True, vmem_limit_bytes=48 * 1024 * 1024
        ),
        cost_estimate=pl.CostEstimate(flops=flops, bytes_accessed=6 << 20, transcendentals=0),
    )(
        tokens,
        query_weight.reshape(width, query_cols),
        key_value_weight.reshape(width, 2 * HEAD_SIZE),
        output_weight,
        cache,
        cosine,
        sine,
        lengths,
        offsets,
        slots,
    )


def solution(mesh):
    return jax.shard_map(
        per_device,
        mesh=mesh,
        in_specs=(
            P("dp", "tx"),
            P(None, "ty", "tx"),
            P(None, "ty", None),
            P("ty", "tx", None),
            P("dp", "ty", None, None),
            P(),
            P(),
            P(),
        ),
        out_specs=(P("dp", ("tx", "ty")), P("dp", "ty", None, None)),
        check_vma=False,
    )
```

```python
import functools
import math

import jax
import jax.numpy as jnp
from jax import lax
from jax.experimental import pallas as pl
from jax.experimental.pallas import tpu as pltpu
from jax.sharding import PartitionSpec as P

HEAD_SIZE = 64
WINDOW_LENGTH = 2048
EPS = 1e-05
LANES = 128
ROW_BLOCK = 128
PROJECT_ROWS = 256
KEY_CHUNK = 512
MESH = pl.DeviceIdType.MESH


def remote(src, dst, send_sem, recv_sem, device):
    return pltpu.make_async_remote_copy(
        src_ref=src, dst_ref=dst, send_sem=send_sem, recv_sem=recv_sem, device_id=device, device_id_type=MESH
    )


def contract_last(left, right):
    return lax.dot_general(left, right, (((1,), (1,)), ((), ())), preferred_element_type=jnp.float32)


def matmul(left, right):
    return jnp.dot(left, right, preferred_element_type=jnp.float32)


def kernel(
    zn, yn,
    tokens, query_weight, key_value_weight, output_weight, cache, lengths_in, offsets_in, slots_in,
    mixed, new_cache,
    lengths, offsets, slots, cosine, sine,
    tok, qw, kvw, old, wbuf, spread, stage, kv, ents, qs, att, score, peak, mine, psend, precv,
    local_sem, t_send, t_recv, w_send, w_recv, s_send, s_recv, g_send, g_recv, h_send, h_recv, e_send, e_recv,
    a_send, a_recv, p_send, p_recv,
):
    me = lax.axis_index("dp")
    tx = lax.axis_index("tx")
    ty = lax.axis_index("ty")
    rows = tok.shape[1]
    half_width = tok.shape[2]
    cols = mixed.shape[1]
    heads = qs.shape[0]
    piece = spread.shape[1]
    blocks = rows // ROW_BLOCK
    sibling = {"tx": 1 - tx}

    def z_peer(d):
        return lax.rem(me + d, zn)

    def y_peer(d):
        return lax.rem(ty + d, yn)

    local = [
        pltpu.make_async_copy(tokens, tok.at[tx], local_sem.at[0]),
        pltpu.make_async_copy(query_weight, qw, local_sem.at[1]),
        pltpu.make_async_copy(key_value_weight, kvw, local_sem.at[2]),
        pltpu.make_async_copy(cache.at[0, 0], old, local_sem.at[3]),
        pltpu.make_async_copy(
            cache.at[0, 0, pl.ds(pl.multiple_of((tx * zn + me) * piece, piece), piece)],
            spread.at[0], local_sem.at[4],
        ),
    ]

    def w_columns(side, block):
        core = tx if side == 0 else 1 - tx
        return output_weight.at[0, :, pl.ds(pl.multiple_of((core * yn + block) * cols, cols), cols)]

    for side in range(2):
        local.append(pltpu.make_async_copy(w_columns(side, ty), wbuf.at[0, side], local_sem.at[5 + side]))
    local.append(pltpu.make_async_copy(lengths_in, lengths, local_sem.at[7]))
    local.append(pltpu.make_async_copy(offsets_in, offsets, local_sem.at[8]))
    local.append(pltpu.make_async_copy(slots_in, slots, local_sem.at[9]))
    for copy in local[7:] + local[:7]:
        copy.start()

    barrier = pltpu.get_barrier_semaphore()
    for d in range(1, zn):
        pl.semaphore_signal(barrier, inc=1, device_id={"dp": z_peer(d)}, device_id_type=MESH)
    for d in range(1, yn):
        pl.semaphore_signal(barrier, inc=1, device_id={"ty": y_peer(d)}, device_id_type=MESH)
    pl.semaphore_signal(barrier, inc=1, device_id=sibling, device_id_type=MESH)
    pl.semaphore_wait(barrier, zn + yn - 1)

    steps = rows // PROJECT_ROWS
    tok_copies = []
    for step in range(steps):
        at = pl.ds(step * PROJECT_ROWS, PROJECT_ROWS)
        tok_copies.append(
            remote(tokens.at[at], tok.at[tx, at], t_send.at[step], t_recv.at[step], sibling)
        )
        tok_copies[-1].start()
    spread_copies = []
    for d in range(1, zn):
        source = cache.at[0, 0, pl.ds(pl.multiple_of((tx * zn + z_peer(d)) * piece, piece), piece)]
        spread_copies.append(
            remote(source, spread.at[d], s_send.at[d], s_recv.at[d], {"dp": z_peer(d)})
        )
        spread_copies[-1].start()
    w_copies = []
    for d in range(1, yn):
        for side in range(2):
            w_copies.append(
                remote(
                    w_columns(side, y_peer(d)), wbuf.at[d, side], w_send.at[d, side], w_recv.at[d, side],
                    {"ty": y_peer(d)},
                )
            )
            w_copies[-1].start()

    for copy in local[7:]:
        copy.wait()
    length = lengths[me]
    offset = offsets[me]

    spot = lax.broadcasted_iota(jnp.int32, (1, LANES), 1)
    freqs = jnp.ones((1, LANES), jnp.float32)
    for m in range(1, HEAD_SIZE // 2):
        freqs = jnp.where(lax.rem(spot, HEAD_SIZE // 2) == m, 10000.0 ** (-2.0 * m / HEAD_SIZE), freqs)
    sign = jnp.where(lax.rem(spot, HEAD_SIZE) < HEAD_SIZE // 2, -1.0, 1.0)

    def tables(step, carry):
        start = pl.multiple_of(step * ROW_BLOCK, ROW_BLOCK)
        position = lax.broadcasted_iota(jnp.int32, (ROW_BLOCK, LANES), 0) + (length + start)
        angles = position.astype(jnp.float32) * freqs
        cosine[pl.ds(start, ROW_BLOCK), :] = jnp.cos(angles)
        sine[pl.ds(start, ROW_BLOCK), :] = jnp.sin(angles) * sign
        return carry

    lax.fori_loop(0, blocks, tables, 0)

    lane = lax.broadcasted_iota(jnp.int32, (PROJECT_ROWS, LANES), 1)
    first_half = lax.rem(lane, HEAD_SIZE) < HEAD_SIZE // 2
    key_lane = lane < HEAD_SIZE

    def project(step):
        at = pl.ds(step * PROJECT_ROWS, PROJECT_ROWS)
        left = tok[0, at, :].astype(jnp.float32)
        right = tok[1, at, :].astype(jnp.float32)
        squares = jnp.sum(left * left + right * right, axis=1, keepdims=True)
        scale = lax.rsqrt(squares * (1.0 / (2 * half_width)) + EPS)
        left = (left * scale).astype(jnp.bfloat16)
        right = (right * scale).astype(jnp.bfloat16)
        queries = matmul(left, qw[:half_width, :]) + matmul(right, qw[half_width:, :])
        pairs = matmul(left, kvw[:half_width, :]) + matmul(right, kvw[half_width:, :])
        cos = cosine[at, :]
        sin = sine[at, :]

        def rotary(u):
            turned = jnp.where(
                first_half,
                pltpu.roll(u, LANES - HEAD_SIZE // 2, 1),
                pltpu.roll(u, HEAD_SIZE // 2, 1),
            )
            return u * cos + turned * sin

        for pair in range(heads // 2):
            rot = rotary(queries[:, pair * LANES : (pair + 1) * LANES]).astype(jnp.bfloat16)
            rot = rot.astype(jnp.float32) * (1.0 / math.sqrt(HEAD_SIZE))
            even = jnp.where(key_lane, rot, 0.0)
            odd = jnp.where(key_lane, pltpu.roll(rot, HEAD_SIZE, 1), 0.0)
            qs[2 * pair, at, :] = even.astype(jnp.bfloat16)
            qs[2 * pair + 1, at, :] = odd.astype(jnp.bfloat16)
        entry = jnp.where(key_lane, rotary(pairs), pairs).astype(jnp.bfloat16)
        kv[pl.ds(WINDOW_LENGTH + step * PROJECT_ROWS, PROJECT_ROWS), :] = entry
        ents[0, at, :] = entry

    local[0].wait()
    local[1].wait()
    local[2].wait()
    tok_copies[0].wait_recv()
    project(0)

    local[4].wait()
    for copy in spread_copies:
        copy.wait_recv()
    def window_rows(core, e):
        quarter = lax.rem(me - e + zn, zn)
        return pl.ds(pl.multiple_of((core * zn + quarter) * piece, piece), piece)

    own_rows = window_rows(tx, 0)
    gather_copies = []
    for e in range(zn):
        slot = slots[z_peer(e)]
        block = spread[lax.rem(me - slot + zn, zn)]
        if e == 0:
            kv[own_rows, :] = block
        else:
            stage[e] = block
            gather_copies.append(
                remote(stage.at[e], kv.at[own_rows], g_send.at[e], g_recv.at[e], {"dp": z_peer(e)})
            )
            gather_copies[-1].start()

    def forward(e):
        here = kv.at[window_rows(tx, e)]
        return remote(here, here, h_send.at[e], h_recv.at[e], sibling)

    forward(0).start()
    for step in range(1, steps):
        tok_copies[step].wait_recv()
        project(step)

    stacked = heads * ROW_BLOCK
    chunks = kv.shape[0] // KEY_CHUNK
    old_chunks = WINDOW_LENGTH // KEY_CHUNK
    slices = KEY_CHUNK // LANES
    part = KEY_CHUNK // 2
    by_piece = piece == part

    def bases(c):
        if by_piece:
            quarter = lax.rem(me - c + zn, zn)
            return [pl.multiple_of((core * zn + quarter) * part, part) for core in range(2)]
        return [c * KEY_CHUNK, c * KEY_CHUNK + part]

    def chunk_rows(c):
        if c >= old_chunks:
            return kv[c * KEY_CHUNK : (c + 1) * KEY_CHUNK, :]
        return jnp.concatenate([kv[pl.ds(base, part), :] for base in bases(c)], axis=0)

    def score_chunk(c, first):
        def one(block, carry):
            start = pl.multiple_of(block * ROW_BLOCK, ROW_BLOCK)
            q = jnp.concatenate([qs[h, pl.ds(start, ROW_BLOCK), :] for h in range(heads)], axis=0)
            row = lax.rem(lax.broadcasted_iota(jnp.int32, (stacked, KEY_CHUNK), 0), ROW_BLOCK) + start
            column = lax.broadcasted_iota(jnp.int32, (1, KEY_CHUNK), 1)
            s = contract_last(q, chunk_rows(c))
            if c < old_chunks:
                low, high = bases(c)
                cycle = jnp.where(column < part, column + low, column + (high - part))
                age = (offset - 1 - cycle) & (WINDOW_LENGTH - 1)
                last = jnp.where(age < length, WINDOW_LENGTH - 2 - age, -1)
                s = jnp.where(row <= last, s, -jnp.inf)
            else:
                s = jnp.where(row >= column + (c - old_chunks) * KEY_CHUNK, s, -jnp.inf)
            score[block, :, c * KEY_CHUNK : (c + 1) * KEY_CHUNK] = s
            top = s[:, :LANES]
            for k in range(1, slices):
                top = jnp.maximum(top, s[:, k * LANES : (k + 1) * LANES])
            if not first:
                top = jnp.maximum(top, peak[block])
            peak[block] = top
            return carry

        lax.fori_loop(0, blocks, one, 0)

    for c in range(old_chunks, chunks):
        score_chunk(c, c == old_chunks)

    entry_copies = []
    for d in range(1, zn):
        entry_copies.append(
            remote(ents.at[0], ents.at[d], e_send.at[d], e_recv.at[d], {"dp": z_peer(d)})
        )
    order = [0, 1, 3, 2] if by_piece else list(range(zn))
    for spot_in_order, e in enumerate(order):
        if spot_in_order + 1 < zn:
            later = order[spot_in_order + 1]
            gather_copies[later - 1].wait_recv()
            forward(later).start()
        else:
            for copy in entry_copies:
                copy.start()
        forward(e).wait_recv()
        if by_piece:
            score_chunk(e, False)
    if not by_piece:
        for c in range(old_chunks):
            score_chunk(c, False)

    def att_copy(block, d):
        at = pl.ds(pl.multiple_of(block * ROW_BLOCK, ROW_BLOCK), ROW_BLOCK)
        return remote(
            att.at[0, at], att.at[d, at], a_send.at[block, d], a_recv.at[block, d], {"ty": y_peer(d)}
        )

    def attend(block, carry):
        start = pl.multiple_of(block * ROW_BLOCK, ROW_BLOCK)
        at = pl.ds(start, ROW_BLOCK)
        top = jnp.max(peak[block], axis=1, keepdims=True)
        total = jnp.zeros((stacked, LANES), jnp.float32)
        summed = jnp.zeros((stacked, LANES), jnp.float32)
        for c in range(chunks):
            powers = jnp.exp(score[block, :, c * KEY_CHUNK : (c + 1) * KEY_CHUNK] - top)
            for k in range(slices):
                total = total + powers[:, k * LANES : (k + 1) * LANES]
            summed = summed + matmul(powers.astype(jnp.bfloat16), chunk_rows(c))
        result = summed / jnp.sum(total, axis=1, keepdims=True)
        low = lax.broadcasted_iota(jnp.int32, (ROW_BLOCK, LANES), 1) < HEAD_SIZE
        for pair in range(heads // 2):
            even = result[2 * pair * ROW_BLOCK : (2 * pair + 1) * ROW_BLOCK, :]
            odd = result[(2 * pair + 1) * ROW_BLOCK : (2 * pair + 2) * ROW_BLOCK, :]
            both = jnp.where(low, pltpu.roll(even, HEAD_SIZE, 1), odd)
            att[0, at, pair * LANES : (pair + 1) * LANES] = both.astype(jnp.bfloat16)
        for d in range(1, yn):
            att_copy(block, d).start()
        return carry

    lax.fori_loop(0, blocks, attend, 0)

    owner = jnp.int32(0)
    turn = jnp.int32(0)
    for r in range(zn):
        here = slots[r] == me
        owner = jnp.where(here, r, owner)
        turn = jnp.where(here, offsets[r], turn)
    for copy in entry_copies:
        copy.wait_recv()
    local[3].wait()
    entry = ents[lax.rem(me - owner + zn, zn)]
    target = lax.broadcasted_iota(jnp.int32, (KEY_CHUNK, rows), 1)
    for c in range(old_chunks):
        at = pl.ds(c * KEY_CHUNK, KEY_CHUNK)
        index = (lax.broadcasted_iota(jnp.int32, (KEY_CHUNK, rows), 0) + (c * KEY_CHUNK - turn)) & (
            WINDOW_LENGTH - 1
        )
        chosen = jnp.where(index == target, 1.0, 0.0).astype(jnp.bfloat16)
        written = matmul(chosen, entry)
        kept = old[at, :].astype(jnp.float32)
        new_cache[0, 0, at, :] = jnp.where(index[:, :LANES] < rows, written, kept).astype(jnp.bfloat16)

    for copy in w_copies:
        copy.wait_recv()
    local[5].wait()
    local[6].wait()
    part_copies = []
    for block in range(blocks):
        at = pl.ds(block * ROW_BLOCK, ROW_BLOCK)
        for d in range(1, yn):
            att_copy(block, d).wait_recv()
        pieces = [att[d, at, :] for d in range(yn)]
        other = matmul(pieces[0], wbuf[0, 1])
        for d in range(1, yn):
            other = other + matmul(pieces[d], wbuf[d, 1])
        psend[at, :] = other
        part_copies.append(
            remote(psend.at[at], precv.at[at], p_send.at[block], p_recv.at[block], sibling)
        )
        part_copies[-1].start()
        own = matmul(pieces[0], wbuf[0, 0])
        for d in range(1, yn):
            own = own + matmul(pieces[d], wbuf[d, 0])
        mine[at, :] = own
    for block in range(blocks):
        at = pl.ds(block * ROW_BLOCK, ROW_BLOCK)
        part_copies[block].wait_recv()
        mixed[at, :] = (mine[at, :] + precv[at, :]).astype(jnp.bfloat16)

    for e in range(zn):
        forward(e).wait_send()
    for copy in tok_copies + spread_copies + w_copies + gather_copies + entry_copies + part_copies:
        copy.wait_send()
    for block in range(blocks):
        for d in range(1, yn):
            att_copy(block, d).wait_send()


def per_device(
    tokens, query_weight, key_value_weight, output_weight, cache, lengths, offsets, slots
):
    zn = lax.axis_size("dp")
    yn = lax.axis_size("ty")
    rows, half_width = tokens.shape
    width = 2 * half_width
    query_cols = query_weight.shape[2]
    heads = query_cols // HEAD_SIZE
    cols = width // (2 * yn)
    piece = WINDOW_LENGTH // (2 * zn)
    blocks = rows // ROW_BLOCK

    bf16 = jnp.bfloat16
    f32 = jnp.float32
    dma = pltpu.SemaphoreType.DMA
    hbm = pl.BlockSpec(memory_space=pltpu.HBM)
    vmem = pl.BlockSpec(memory_space=pltpu.VMEM)
    flops = 2 * rows * (width * (query_cols + 2 * HEAD_SIZE + width // yn) + 4 * query_cols * (WINDOW_LENGTH + rows))
    return pl.pallas_call(
        functools.partial(kernel, zn, yn),
        out_shape=(
            jax.ShapeDtypeStruct((rows, cols), bf16),
            jax.ShapeDtypeStruct(cache.shape, bf16),
        ),
        in_specs=[hbm] * 8,
        out_specs=(vmem, vmem),
        scratch_shapes=[
            pltpu.SMEM(lengths.shape, jnp.int32),
            pltpu.SMEM(offsets.shape, jnp.int32),
            pltpu.SMEM(slots.shape, jnp.int32),
            pltpu.VMEM((rows, LANES), f32),
            pltpu.VMEM((rows, LANES), f32),
            pltpu.VMEM((2, rows, half_width), bf16),
            pltpu.VMEM((width, query_cols), bf16),
            pltpu.VMEM((width, 2 * HEAD_SIZE), bf16),
            pltpu.VMEM((WINDOW_LENGTH, 2 * HEAD_SIZE), bf16),
            pltpu.VMEM((yn, 2, query_cols, cols), bf16),
            pltpu.VMEM((zn, piece, 2 * HEAD_SIZE), bf16),
            pltpu.VMEM((zn, piece, 2 * HEAD_SIZE), bf16),
            pltpu.VMEM((WINDOW_LENGTH + rows, 2 * HEAD_SIZE), bf16),
            pltpu.VMEM((zn, rows, 2 * HEAD_SIZE), bf16),
            pltpu.VMEM((heads, rows, LANES), bf16),
            pltpu.VMEM((yn, rows, query_cols), bf16),
            pltpu.VMEM((blocks, heads * ROW_BLOCK, WINDOW_LENGTH + rows), f32),
            pltpu.VMEM((blocks, heads * ROW_BLOCK, LANES), f32),
            pltpu.VMEM((rows, cols), f32),
            pltpu.VMEM((rows, cols), f32),
            pltpu.VMEM((rows, cols), f32),
            dma((10,)),
            dma((rows // PROJECT_ROWS,)),
            dma((rows // PROJECT_ROWS,)),
            dma((yn, 2)),
            dma((yn, 2)),
            dma((zn,)),
            dma((zn,)),
            dma((zn,)),
            dma((zn,)),
            dma((zn,)),
            dma((zn,)),
            dma((zn,)),
            dma((zn,)),
            dma((blocks, yn)),
            dma((blocks, yn)),
            dma((blocks,)),
            dma((blocks,)),
        ],
        compiler_params=pltpu.CompilerParams(
            collective_id=0, has_side_effects=True, vmem_limit_bytes=46 * 1024 * 1024
        ),
        cost_estimate=pl.CostEstimate(flops=flops, bytes_accessed=6 << 20, transcendentals=0),
    )(
        tokens,
        query_weight.reshape(width, query_cols),
        key_value_weight.reshape(width, 2 * HEAD_SIZE),
        output_weight,
        cache,
        lengths,
        offsets,
        slots,
    )


def solution(mesh):
    return jax.shard_map(
        per_device,
        mesh=mesh,
        in_specs=(
            P("dp", "tx"),
            P(None, "ty", "tx"),
            P(None, "ty", None),
            P("ty", "tx", None),
            P("dp", "ty", None, None),
            P(),
            P(),
            P(),
        ),
        out_specs=(P("dp", ("tx", "ty")), P("dp", "ty", None, None)),
        check_vma=False,
    )
```

```python
import functools
import math

import jax
import jax.numpy as jnp
from jax import lax
from jax.experimental import pallas as pl
from jax.experimental.pallas import tpu as pltpu
from jax.sharding import PartitionSpec as P

HEAD_SIZE = 64
WINDOW_LENGTH = 2048
EPS = 1e-05
LANES = 128
ROW_BLOCK = 128
PROJECT_ROWS = 256
KEY_CHUNK = 512
MESH = pl.DeviceIdType.MESH


def remote(src, dst, send_sem, recv_sem, device):
    return pltpu.make_async_remote_copy(
        src_ref=src, dst_ref=dst, send_sem=send_sem, recv_sem=recv_sem, device_id=device, device_id_type=MESH
    )


def contract_last(left, right):
    return lax.dot_general(left, right, (((1,), (1,)), ((), ())), preferred_element_type=jnp.float32)


def matmul(left, right):
    return jnp.dot(left, right, preferred_element_type=jnp.float32)


def kernel(
    zn, yn,
    tokens, query_weight, key_value_weight, output_weight, cache, lengths_in, offsets_in, slots_in,
    mixed, new_cache,
    lengths, offsets, slots, cosine, sine,
    tok, qw, kvw, old, wbuf, spread, stage, kv, ents, qs, att, score, peak, mine, psend, precv,
    local_sem, t_send, t_recv, w_send, w_recv, s_send, s_recv, g_send, g_recv, h_send, h_recv, e_send, e_recv,
    a_send, a_recv, p_send, p_recv,
):
    me = lax.axis_index("dp")
    tx = lax.axis_index("tx")
    ty = lax.axis_index("ty")
    rows = tok.shape[1]
    half_width = tok.shape[2]
    cols = mixed.shape[1]
    heads = qs.shape[0]
    piece = spread.shape[1]
    blocks = rows // ROW_BLOCK
    sibling = {"tx": 1 - tx}

    def z_peer(d):
        return lax.rem(me + d, zn)

    def y_peer(d):
        return lax.rem(ty + d, yn)

    local = [
        pltpu.make_async_copy(tokens, tok.at[tx], local_sem.at[0]),
        pltpu.make_async_copy(query_weight, qw, local_sem.at[1]),
        pltpu.make_async_copy(key_value_weight, kvw, local_sem.at[2]),
        pltpu.make_async_copy(cache.at[0, 0], old, local_sem.at[3]),
        pltpu.make_async_copy(
            cache.at[0, 0, pl.ds(pl.multiple_of((tx * zn + me) * piece, piece), piece)],
            spread.at[0], local_sem.at[4],
        ),
    ]

    def w_columns(side, block):
        core = tx if side == 0 else 1 - tx
        return output_weight.at[0, :, pl.ds(pl.multiple_of((core * yn + block) * cols, cols), cols)]

    for side in range(2):
        local.append(pltpu.make_async_copy(w_columns(side, ty), wbuf.at[0, side], local_sem.at[5 + side]))
    local.append(pltpu.make_async_copy(lengths_in, lengths, local_sem.at[7]))
    local.append(pltpu.make_async_copy(offsets_in, offsets, local_sem.at[8]))
    local.append(pltpu.make_async_copy(slots_in, slots, local_sem.at[9]))
    for copy in local[7:] + local[:7]:
        copy.start()

    barrier = pltpu.get_barrier_semaphore()
    for d in range(1, zn):
        pl.semaphore_signal(barrier, inc=1, device_id={"dp": z_peer(d)}, device_id_type=MESH)
    for d in range(1, yn):
        pl.semaphore_signal(barrier, inc=1, device_id={"ty": y_peer(d)}, device_id_type=MESH)
    pl.semaphore_signal(barrier, inc=1, device_id=sibling, device_id_type=MESH)
    pl.semaphore_wait(barrier, zn + yn - 1)

    steps = rows // PROJECT_ROWS
    tok_copies = []
    for step in range(steps):
        at = pl.ds(step * PROJECT_ROWS, PROJECT_ROWS)
        tok_copies.append(
            remote(tokens.at[at], tok.at[tx, at], t_send.at[step], t_recv.at[step], sibling)
        )
        tok_copies[-1].start()
    spread_copies = []
    for d in range(1, zn):
        source = cache.at[0, 0, pl.ds(pl.multiple_of((tx * zn + z_peer(d)) * piece, piece), piece)]
        spread_copies.append(
            remote(source, spread.at[d], s_send.at[d], s_recv.at[d], {"dp": z_peer(d)})
        )
        spread_copies[-1].start()
    w_copies = []
    for d in range(1, yn):
        for side in range(2):
            w_copies.append(
                remote(
                    w_columns(side, y_peer(d)), wbuf.at[d, side], w_send.at[d, side], w_recv.at[d, side],
                    {"ty": y_peer(d)},
                )
            )
            w_copies[-1].start()

    for copy in local[7:]:
        copy.wait()
    length = lengths[me]
    offset = offsets[me]

    spot = lax.broadcasted_iota(jnp.int32, (1, LANES), 1)
    freqs = jnp.ones((1, LANES), jnp.float32)
    for m in range(1, HEAD_SIZE // 2):
        freqs = jnp.where(lax.rem(spot, HEAD_SIZE // 2) == m, 10000.0 ** (-2.0 * m / HEAD_SIZE), freqs)
    sign = jnp.where(lax.rem(spot, HEAD_SIZE) < HEAD_SIZE // 2, -1.0, 1.0)

    def tables(step, carry):
        start = pl.multiple_of(step * ROW_BLOCK, ROW_BLOCK)
        position = lax.broadcasted_iota(jnp.int32, (ROW_BLOCK, LANES), 0) + (length + start)
        angles = position.astype(jnp.float32) * freqs
        cosine[pl.ds(start, ROW_BLOCK), :] = jnp.cos(angles)
        sine[pl.ds(start, ROW_BLOCK), :] = jnp.sin(angles) * sign
        return carry

    lax.fori_loop(0, blocks, tables, 0)

    lane = lax.broadcasted_iota(jnp.int32, (PROJECT_ROWS, LANES), 1)
    first_half = lax.rem(lane, HEAD_SIZE) < HEAD_SIZE // 2
    key_lane = lane < HEAD_SIZE

    def project(step):
        at = pl.ds(step * PROJECT_ROWS, PROJECT_ROWS)
        left = tok[0, at, :].astype(jnp.float32)
        right = tok[1, at, :].astype(jnp.float32)
        squares = jnp.sum(left * left + right * right, axis=1, keepdims=True)
        scale = lax.rsqrt(squares * (1.0 / (2 * half_width)) + EPS)
        left = (left * scale).astype(jnp.bfloat16)
        right = (right * scale).astype(jnp.bfloat16)
        queries = matmul(left, qw[:half_width, :]) + matmul(right, qw[half_width:, :])
        pairs = matmul(left, kvw[:half_width, :]) + matmul(right, kvw[half_width:, :])
        cos = cosine[at, :]
        sin = sine[at, :]

        def rotary(u):
            turned = jnp.where(
                first_half,
                pltpu.roll(u, LANES - HEAD_SIZE // 2, 1),
                pltpu.roll(u, HEAD_SIZE // 2, 1),
            )
            return u * cos + turned * sin

        for pair in range(heads // 2):
            rot = rotary(queries[:, pair * LANES : (pair + 1) * LANES]).astype(jnp.bfloat16)
            rot = rot.astype(jnp.float32) * (1.0 / math.sqrt(HEAD_SIZE))
            even = jnp.where(key_lane, rot, 0.0)
            odd = jnp.where(key_lane, pltpu.roll(rot, HEAD_SIZE, 1), 0.0)
            qs[2 * pair, at, :] = even.astype(jnp.bfloat16)
            qs[2 * pair + 1, at, :] = odd.astype(jnp.bfloat16)
        entry = jnp.where(key_lane, rotary(pairs), pairs).astype(jnp.bfloat16)
        kv[pl.ds(WINDOW_LENGTH + step * PROJECT_ROWS, PROJECT_ROWS), :] = entry
        ents[0, at, :] = entry

    local[0].wait()
    local[1].wait()
    local[2].wait()
    tok_copies[0].wait_recv()
    project(0)

    local[4].wait()
    for copy in spread_copies:
        copy.wait_recv()
    def window_rows(core, e):
        quarter = lax.rem(me - e + zn, zn)
        return pl.ds(pl.multiple_of((core * zn + quarter) * piece, piece), piece)

    own_rows = window_rows(tx, 0)
    gather_copies = []
    for e in range(zn):
        slot = slots[z_peer(e)]
        block = spread[lax.rem(me - slot + zn, zn)]
        if e == 0:
            kv[own_rows, :] = block
        else:
            stage[e] = block
            gather_copies.append(
                remote(stage.at[e], kv.at[own_rows], g_send.at[e], g_recv.at[e], {"dp": z_peer(e)})
            )
            gather_copies[-1].start()

    def forward(e):
        here = kv.at[window_rows(tx, e)]
        return remote(here, here, h_send.at[e], h_recv.at[e], sibling)

    forward(0).start()
    for step in range(1, steps):
        tok_copies[step].wait_recv()
        project(step)

    stacked = heads * ROW_BLOCK
    chunks = kv.shape[0] // KEY_CHUNK
    old_chunks = WINDOW_LENGTH // KEY_CHUNK
    slices = KEY_CHUNK // LANES
    part = KEY_CHUNK // 2
    by_piece = piece == part

    def bases(c):
        if by_piece:
            quarter = lax.rem(me - c + zn, zn)
            return [pl.multiple_of((core * zn + quarter) * part, part) for core in range(2)]
        return [c * KEY_CHUNK, c * KEY_CHUNK + part]

    def chunk_rows(c):
        if c >= old_chunks:
            return kv[c * KEY_CHUNK : (c + 1) * KEY_CHUNK, :]
        return jnp.concatenate([kv[pl.ds(base, part), :] for base in bases(c)], axis=0)

    def score_chunk(c, first):
        def one(block, carry):
            start = pl.multiple_of(block * ROW_BLOCK, ROW_BLOCK)
            q = jnp.concatenate([qs[h, pl.ds(start, ROW_BLOCK), :] for h in range(heads)], axis=0)
            row = lax.broadcasted_iota(jnp.int32, (ROW_BLOCK, KEY_CHUNK), 0) + start
            column = lax.broadcasted_iota(jnp.int32, (1, KEY_CHUNK), 1)
            if c < old_chunks:
                low, high = bases(c)
                cycle = jnp.where(column < part, column + low, column + (high - part))
                age = (offset - 1 - cycle) & (WINDOW_LENGTH - 1)
                last = jnp.where(age < length, WINDOW_LENGTH - 2 - age, -1)
                bias = jnp.where(row <= last, 0.0, -jnp.inf)
            else:
                bias = jnp.where(row >= column + (c - old_chunks) * KEY_CHUNK, 0.0, -jnp.inf)
            s = contract_last(q, chunk_rows(c))
            for h in range(heads):
                at = pl.ds(h * ROW_BLOCK, ROW_BLOCK)
                mine_s = s[h * ROW_BLOCK : (h + 1) * ROW_BLOCK, :] + bias
                score[block, at, c * KEY_CHUNK : (c + 1) * KEY_CHUNK] = mine_s
                top = mine_s[:, :LANES]
                for k in range(1, slices):
                    top = jnp.maximum(top, mine_s[:, k * LANES : (k + 1) * LANES])
                if not first:
                    top = jnp.maximum(top, peak[block, at, :])
                peak[block, at, :] = top
            return carry

        lax.fori_loop(0, blocks, one, 0)

    for c in range(old_chunks, chunks):
        score_chunk(c, c == old_chunks)

    entry_copies = []
    for d in range(1, zn):
        entry_copies.append(
            remote(ents.at[0], ents.at[d], e_send.at[d], e_recv.at[d], {"dp": z_peer(d)})
        )
    order = [0, 1, 3, 2] if by_piece else list(range(zn))
    for spot_in_order, e in enumerate(order):
        if spot_in_order + 1 < zn:
            later = order[spot_in_order + 1]
            gather_copies[later - 1].wait_recv()
            forward(later).start()
        else:
            for copy in entry_copies:
                copy.start()
        forward(e).wait_recv()
        if by_piece:
            score_chunk(e, False)
    if not by_piece:
        for c in range(old_chunks):
            score_chunk(c, False)

    def att_copy(block, d):
        at = pl.ds(pl.multiple_of(block * ROW_BLOCK, ROW_BLOCK), ROW_BLOCK)
        return remote(
            att.at[0, at], att.at[d, at], a_send.at[block, d], a_recv.at[block, d], {"ty": y_peer(d)}
        )

    def attend(block, carry):
        start = pl.multiple_of(block * ROW_BLOCK, ROW_BLOCK)
        at = pl.ds(start, ROW_BLOCK)
        top = jnp.max(peak[block], axis=1, keepdims=True)
        total = jnp.zeros((stacked, LANES), jnp.float32)
        summed = jnp.zeros((stacked, LANES), jnp.float32)
        for c in range(chunks):
            powers = jnp.exp(score[block, :, c * KEY_CHUNK : (c + 1) * KEY_CHUNK] - top)
            for k in range(slices):
                total = total + powers[:, k * LANES : (k + 1) * LANES]
            summed = summed + matmul(powers.astype(jnp.bfloat16), chunk_rows(c))
        result = summed / jnp.sum(total, axis=1, keepdims=True)
        low = lax.broadcasted_iota(jnp.int32, (ROW_BLOCK, LANES), 1) < HEAD_SIZE
        for pair in range(heads // 2):
            even = result[2 * pair * ROW_BLOCK : (2 * pair + 1) * ROW_BLOCK, :]
            odd = result[(2 * pair + 1) * ROW_BLOCK : (2 * pair + 2) * ROW_BLOCK, :]
            both = jnp.where(low, pltpu.roll(even, HEAD_SIZE, 1), odd)
            att[0, at, pair * LANES : (pair + 1) * LANES] = both.astype(jnp.bfloat16)
        for d in range(1, yn):
            att_copy(block, d).start()
        return carry

    lax.fori_loop(0, blocks, attend, 0)

    owner = jnp.int32(0)
    turn = jnp.int32(0)
    for r in range(zn):
        here = slots[r] == me
        owner = jnp.where(here, r, owner)
        turn = jnp.where(here, offsets[r], turn)
    for copy in entry_copies:
        copy.wait_recv()
    local[3].wait()
    entry = ents[lax.rem(me - owner + zn, zn)]
    target = lax.broadcasted_iota(jnp.int32, (KEY_CHUNK, rows), 1)
    for c in range(old_chunks):
        at = pl.ds(c * KEY_CHUNK, KEY_CHUNK)
        index = (lax.broadcasted_iota(jnp.int32, (KEY_CHUNK, rows), 0) + (c * KEY_CHUNK - turn)) & (
            WINDOW_LENGTH - 1
        )
        chosen = jnp.where(index == target, 1.0, 0.0).astype(jnp.bfloat16)
        written = matmul(chosen, entry)
        kept = old[at, :].astype(jnp.float32)
        new_cache[0, 0, at, :] = jnp.where(index[:, :LANES] < rows, written, kept).astype(jnp.bfloat16)

    for copy in w_copies:
        copy.wait_recv()
    local[5].wait()
    local[6].wait()
    part_copies = []
    for block in range(blocks):
        at = pl.ds(block * ROW_BLOCK, ROW_BLOCK)
        for d in range(1, yn):
            att_copy(block, d).wait_recv()
        pieces = [att[d, at, :] for d in range(yn)]
        other = matmul(pieces[0], wbuf[0, 1])
        for d in range(1, yn):
            other = other + matmul(pieces[d], wbuf[d, 1])
        psend[at, :] = other
        part_copies.append(
            remote(psend.at[at], precv.at[at], p_send.at[block], p_recv.at[block], sibling)
        )
        part_copies[-1].start()
        own = matmul(pieces[0], wbuf[0, 0])
        for d in range(1, yn):
            own = own + matmul(pieces[d], wbuf[d, 0])
        mine[at, :] = own
    for block in range(blocks):
        at = pl.ds(block * ROW_BLOCK, ROW_BLOCK)
        part_copies[block].wait_recv()
        mixed[at, :] = (mine[at, :] + precv[at, :]).astype(jnp.bfloat16)

    for e in range(zn):
        forward(e).wait_send()
    for copy in tok_copies + spread_copies + w_copies + gather_copies + entry_copies + part_copies:
        copy.wait_send()
    for block in range(blocks):
        for d in range(1, yn):
            att_copy(block, d).wait_send()


def per_device(
    tokens, query_weight, key_value_weight, output_weight, cache, lengths, offsets, slots
):
    zn = lax.axis_size("dp")
    yn = lax.axis_size("ty")
    rows, half_width = tokens.shape
    width = 2 * half_width
    query_cols = query_weight.shape[2]
    heads = query_cols // HEAD_SIZE
    cols = width // (2 * yn)
    piece = WINDOW_LENGTH // (2 * zn)
    blocks = rows // ROW_BLOCK

    bf16 = jnp.bfloat16
    f32 = jnp.float32
    dma = pltpu.SemaphoreType.DMA
    hbm = pl.BlockSpec(memory_space=pltpu.HBM)
    vmem = pl.BlockSpec(memory_space=pltpu.VMEM)
    flops = 2 * rows * (width * (query_cols + 2 * HEAD_SIZE + width // yn) + 4 * query_cols * (WINDOW_LENGTH + rows))
    return pl.pallas_call(
        functools.partial(kernel, zn, yn),
        out_shape=(
            jax.ShapeDtypeStruct((rows, cols), bf16),
            jax.ShapeDtypeStruct(cache.shape, bf16),
        ),
        in_specs=[hbm] * 8,
        out_specs=(vmem, vmem),
        scratch_shapes=[
            pltpu.SMEM(lengths.shape, jnp.int32),
            pltpu.SMEM(offsets.shape, jnp.int32),
            pltpu.SMEM(slots.shape, jnp.int32),
            pltpu.VMEM((rows, LANES), f32),
            pltpu.VMEM((rows, LANES), f32),
            pltpu.VMEM((2, rows, half_width), bf16),
            pltpu.VMEM((width, query_cols), bf16),
            pltpu.VMEM((width, 2 * HEAD_SIZE), bf16),
            pltpu.VMEM((WINDOW_LENGTH, 2 * HEAD_SIZE), bf16),
            pltpu.VMEM((yn, 2, query_cols, cols), bf16),
            pltpu.VMEM((zn, piece, 2 * HEAD_SIZE), bf16),
            pltpu.VMEM((zn, piece, 2 * HEAD_SIZE), bf16),
            pltpu.VMEM((WINDOW_LENGTH + rows, 2 * HEAD_SIZE), bf16),
            pltpu.VMEM((zn, rows, 2 * HEAD_SIZE), bf16),
            pltpu.VMEM((heads, rows, LANES), bf16),
            pltpu.VMEM((yn, rows, query_cols), bf16),
            pltpu.VMEM((blocks, heads * ROW_BLOCK, WINDOW_LENGTH + rows), f32),
            pltpu.VMEM((blocks, heads * ROW_BLOCK, LANES), f32),
            pltpu.VMEM((rows, cols), f32),
            pltpu.VMEM((rows, cols), f32),
            pltpu.VMEM((rows, cols), f32),
            dma((10,)),
            dma((rows // PROJECT_ROWS,)),
            dma((rows // PROJECT_ROWS,)),
            dma((yn, 2)),
            dma((yn, 2)),
            dma((zn,)),
            dma((zn,)),
            dma((zn,)),
            dma((zn,)),
            dma((zn,)),
            dma((zn,)),
            dma((zn,)),
            dma((zn,)),
            dma((blocks, yn)),
            dma((blocks, yn)),
            dma((blocks,)),
            dma((blocks,)),
        ],
        compiler_params=pltpu.CompilerParams(
            collective_id=0, has_side_effects=True, vmem_limit_bytes=56 * 1024 * 1024
        ),
        cost_estimate=pl.CostEstimate(flops=flops, bytes_accessed=6 << 20, transcendentals=0),
    )(
        tokens,
        query_weight.reshape(width, query_cols),
        key_value_weight.reshape(width, 2 * HEAD_SIZE),
        output_weight,
        cache,
        lengths,
        offsets,
        slots,
    )


def solution(mesh):
    return jax.shard_map(
        per_device,
        mesh=mesh,
        in_specs=(
            P("dp", "tx"),
            P(None, "ty", "tx"),
            P(None, "ty", None),
            P("ty", "tx", None),
            P("dp", "ty", None, None),
            P(),
            P(),
            P(),
        ),
        out_specs=(P("dp", ("tx", "ty")), P("dp", "ty", None, None)),
        check_vma=False,
    )
```

```python
import functools
import math

import jax
import jax.numpy as jnp
from jax import lax
from jax.experimental import pallas as pl
from jax.experimental.pallas import tpu as pltpu
from jax.sharding import PartitionSpec as P

HEAD_SIZE = 64
WINDOW_LENGTH = 2048
EPS = 1e-05
LANES = 128
ROW_BLOCK = 128
PROJECT_ROWS = 256
KEY_CHUNK = 512
MESH = pl.DeviceIdType.MESH


def remote(src, dst, send_sem, recv_sem, device):
    return pltpu.make_async_remote_copy(
        src_ref=src, dst_ref=dst, send_sem=send_sem, recv_sem=recv_sem, device_id=device, device_id_type=MESH
    )


def contract_last(left, right):
    return lax.dot_general(left, right, (((1,), (1,)), ((), ())), preferred_element_type=jnp.float32)


def matmul(left, right):
    return jnp.dot(left, right, preferred_element_type=jnp.float32)


def kernel(
    zn, yn,
    tokens, query_weight, key_value_weight, output_weight, cache, lengths_in, offsets_in, slots_in,
    mixed, new_cache,
    lengths, offsets, slots, cosine, sine,
    tok, qw, kvw, old, wbuf, spread, stage, kv, ents, qs, att, score, peak, mine, psend, precv,
    local_sem, t_send, t_recv, w_send, w_recv, s_send, s_recv, g_send, g_recv, h_send, h_recv, e_send, e_recv,
    a_send, a_recv, p_send, p_recv,
):
    me = lax.axis_index("dp")
    tx = lax.axis_index("tx")
    ty = lax.axis_index("ty")
    rows = tok.shape[1]
    half_width = tok.shape[2]
    cols = mixed.shape[1]
    heads = qs.shape[0]
    piece = spread.shape[1]
    blocks = rows // ROW_BLOCK
    sibling = {"tx": 1 - tx}

    def z_peer(d):
        return lax.rem(me + d, zn)

    def y_peer(d):
        return lax.rem(ty + d, yn)

    local = [
        pltpu.make_async_copy(tokens, tok.at[tx], local_sem.at[0]),
        pltpu.make_async_copy(query_weight, qw, local_sem.at[1]),
        pltpu.make_async_copy(key_value_weight, kvw, local_sem.at[2]),
        pltpu.make_async_copy(cache.at[0, 0], old, local_sem.at[3]),
        pltpu.make_async_copy(
            cache.at[0, 0, pl.ds(pl.multiple_of((tx * zn + me) * piece, piece), piece)],
            spread.at[0], local_sem.at[4],
        ),
    ]

    def w_columns(side, block):
        core = tx if side == 0 else 1 - tx
        return output_weight.at[0, :, pl.ds(pl.multiple_of((core * yn + block) * cols, cols), cols)]

    for side in range(2):
        local.append(pltpu.make_async_copy(w_columns(side, ty), wbuf.at[0, side], local_sem.at[5 + side]))
    local.append(pltpu.make_async_copy(lengths_in, lengths, local_sem.at[7]))
    local.append(pltpu.make_async_copy(offsets_in, offsets, local_sem.at[8]))
    local.append(pltpu.make_async_copy(slots_in, slots, local_sem.at[9]))
    for copy in local[7:] + local[:7]:
        copy.start()

    barrier = pltpu.get_barrier_semaphore()
    for d in range(1, zn):
        pl.semaphore_signal(barrier, inc=1, device_id={"dp": z_peer(d)}, device_id_type=MESH)
    for d in range(1, yn):
        pl.semaphore_signal(barrier, inc=1, device_id={"ty": y_peer(d)}, device_id_type=MESH)
    pl.semaphore_signal(barrier, inc=1, device_id=sibling, device_id_type=MESH)
    pl.semaphore_wait(barrier, zn + yn - 1)

    steps = rows // PROJECT_ROWS
    tok_copies = []
    for step in range(steps):
        at = pl.ds(step * PROJECT_ROWS, PROJECT_ROWS)
        tok_copies.append(
            remote(tokens.at[at], tok.at[tx, at], t_send.at[step], t_recv.at[step], sibling)
        )
        tok_copies[-1].start()
    spread_copies = []
    for d in range(1, zn):
        source = cache.at[0, 0, pl.ds(pl.multiple_of((tx * zn + z_peer(d)) * piece, piece), piece)]
        spread_copies.append(
            remote(source, spread.at[d], s_send.at[d], s_recv.at[d], {"dp": z_peer(d)})
        )
        spread_copies[-1].start()
    w_copies = []
    for d in range(1, yn):
        for side in range(2):
            w_copies.append(
                remote(
                    w_columns(side, y_peer(d)), wbuf.at[d, side], w_send.at[d, side], w_recv.at[d, side],
                    {"ty": y_peer(d)},
                )
            )
            w_copies[-1].start()

    for copy in local[7:]:
        copy.wait()
    length = lengths[me]
    offset = offsets[me]

    spot = lax.broadcasted_iota(jnp.int32, (1, LANES), 1)
    freqs = jnp.ones((1, LANES), jnp.float32)
    for m in range(1, HEAD_SIZE // 2):
        freqs = jnp.where(lax.rem(spot, HEAD_SIZE // 2) == m, 10000.0 ** (-2.0 * m / HEAD_SIZE), freqs)
    sign = jnp.where(lax.rem(spot, HEAD_SIZE) < HEAD_SIZE // 2, -1.0, 1.0)

    def tables(step, carry):
        start = pl.multiple_of(step * ROW_BLOCK, ROW_BLOCK)
        position = lax.broadcasted_iota(jnp.int32, (ROW_BLOCK, LANES), 0) + (length + start)
        angles = position.astype(jnp.float32) * freqs
        cosine[pl.ds(start, ROW_BLOCK), :] = jnp.cos(angles)
        sine[pl.ds(start, ROW_BLOCK), :] = jnp.sin(angles) * sign
        return carry

    lax.fori_loop(0, blocks, tables, 0)

    lane = lax.broadcasted_iota(jnp.int32, (PROJECT_ROWS, LANES), 1)
    first_half = lax.rem(lane, HEAD_SIZE) < HEAD_SIZE // 2
    key_lane = lane < HEAD_SIZE

    def project(step):
        at = pl.ds(step * PROJECT_ROWS, PROJECT_ROWS)
        left = tok[0, at, :].astype(jnp.float32)
        right = tok[1, at, :].astype(jnp.float32)
        squares = jnp.sum(left * left + right * right, axis=1, keepdims=True)
        scale = lax.rsqrt(squares * (1.0 / (2 * half_width)) + EPS)
        left = (left * scale).astype(jnp.bfloat16)
        right = (right * scale).astype(jnp.bfloat16)
        queries = matmul(left, qw[:half_width, :]) + matmul(right, qw[half_width:, :])
        pairs = matmul(left, kvw[:half_width, :]) + matmul(right, kvw[half_width:, :])
        cos = cosine[at, :]
        sin = sine[at, :]

        def rotary(u):
            turned = jnp.where(
                first_half,
                pltpu.roll(u, LANES - HEAD_SIZE // 2, 1),
                pltpu.roll(u, HEAD_SIZE // 2, 1),
            )
            return u * cos + turned * sin

        for pair in range(heads // 2):
            rot = rotary(queries[:, pair * LANES : (pair + 1) * LANES]).astype(jnp.bfloat16)
            rot = rot.astype(jnp.float32) * (1.0 / math.sqrt(HEAD_SIZE))
            even = jnp.where(key_lane, rot, 0.0)
            odd = jnp.where(key_lane, pltpu.roll(rot, HEAD_SIZE, 1), 0.0)
            qs[2 * pair, at, :] = even.astype(jnp.bfloat16)
            qs[2 * pair + 1, at, :] = odd.astype(jnp.bfloat16)
        entry = jnp.where(key_lane, rotary(pairs), pairs).astype(jnp.bfloat16)
        kv[pl.ds(WINDOW_LENGTH + step * PROJECT_ROWS, PROJECT_ROWS), :] = entry
        ents[0, at, :] = entry

    local[0].wait()
    local[1].wait()
    local[2].wait()
    tok_copies[0].wait_recv()
    project(0)

    local[4].wait()
    for copy in spread_copies:
        copy.wait_recv()
    def window_rows(core, e):
        quarter = lax.rem(me - e + zn, zn)
        return pl.ds(pl.multiple_of((core * zn + quarter) * piece, piece), piece)

    own_rows = window_rows(tx, 0)
    gather_copies = []
    for e in range(zn):
        slot = slots[z_peer(e)]
        block = spread[lax.rem(me - slot + zn, zn)]
        if e == 0:
            kv[own_rows, :] = block
        else:
            stage[e] = block
            gather_copies.append(
                remote(stage.at[e], kv.at[own_rows], g_send.at[e], g_recv.at[e], {"dp": z_peer(e)})
            )
            gather_copies[-1].start()

    def forward(e):
        here = kv.at[window_rows(tx, e)]
        return remote(here, here, h_send.at[e], h_recv.at[e], sibling)

    forward(0).start()
    for step in range(1, steps):
        tok_copies[step].wait_recv()
        project(step)

    stacked = heads * ROW_BLOCK
    chunks = kv.shape[0] // KEY_CHUNK
    old_chunks = WINDOW_LENGTH // KEY_CHUNK
    slices = KEY_CHUNK // LANES
    part = KEY_CHUNK // 2
    by_piece = piece == part

    def bases(c):
        if by_piece:
            quarter = lax.rem(me - c + zn, zn)
            return [pl.multiple_of((core * zn + quarter) * part, part) for core in range(2)]
        return [c * KEY_CHUNK, c * KEY_CHUNK + part]

    def chunk_rows(c):
        if c >= old_chunks:
            return kv[c * KEY_CHUNK : (c + 1) * KEY_CHUNK, :]
        return jnp.concatenate([kv[pl.ds(base, part), :] for base in bases(c)], axis=0)

    def score_block(c, first):
        def one(block, carry):
            start = pl.multiple_of(block * ROW_BLOCK, ROW_BLOCK)
            q = jnp.concatenate([qs[h, pl.ds(start, ROW_BLOCK), :] for h in range(heads)], axis=0)
            row = lax.broadcasted_iota(jnp.int32, (ROW_BLOCK, KEY_CHUNK), 0) + start
            column = lax.broadcasted_iota(jnp.int32, (1, KEY_CHUNK), 1)
            if c < old_chunks:
                low, high = bases(c)
                cycle = jnp.where(column < part, column + low, column + (high - part))
                age = (offset - 1 - cycle) & (WINDOW_LENGTH - 1)
                last = jnp.where(age < length, WINDOW_LENGTH - 2 - age, -1)
                bias = jnp.where(row <= last, 0.0, -jnp.inf)
            else:
                bias = jnp.where(row >= column + (c - old_chunks) * KEY_CHUNK, 0.0, -jnp.inf)
            s = contract_last(q, chunk_rows(c))
            for h in range(heads):
                at = pl.ds(h * ROW_BLOCK, ROW_BLOCK)
                mine_s = s[h * ROW_BLOCK : (h + 1) * ROW_BLOCK, :] + bias
                score[block, at, c * KEY_CHUNK : (c + 1) * KEY_CHUNK] = mine_s
                top = mine_s[:, :LANES]
                for k in range(1, slices):
                    top = jnp.maximum(top, mine_s[:, k * LANES : (k + 1) * LANES])
                if not first:
                    top = jnp.maximum(top, peak[block, at, :])
                peak[block, at, :] = top
            return carry

        return one

    def score_chunk(c, first):
        lax.fori_loop(0, blocks, score_block(c, first), 0)

    for c in range(old_chunks, chunks):
        score_chunk(c, c == old_chunks)

    entry_copies = []
    for d in range(1, zn):
        entry_copies.append(
            remote(ents.at[0], ents.at[d], e_send.at[d], e_recv.at[d], {"dp": z_peer(d)})
        )
    order = [0, 1, 3, 2] if by_piece else list(range(zn))
    for spot_in_order, e in enumerate(order):
        if spot_in_order + 1 < zn:
            later = order[spot_in_order + 1]
            gather_copies[later - 1].wait_recv()
            forward(later).start()
        else:
            for copy in entry_copies:
                copy.start()
        forward(e).wait_recv()
        if by_piece and spot_in_order + 1 < zn:
            score_chunk(e, False)
    final_chunk = order[-1] if by_piece else old_chunks - 1
    if not by_piece:
        for c in range(old_chunks - 1):
            score_chunk(c, False)

    def att_copy(block, d):
        at = pl.ds(pl.multiple_of(block * ROW_BLOCK, ROW_BLOCK), ROW_BLOCK)
        return remote(
            att.at[0, at], att.at[d, at], a_send.at[block, d], a_recv.at[block, d], {"ty": y_peer(d)}
        )

    def attend(block, carry):
        start = pl.multiple_of(block * ROW_BLOCK, ROW_BLOCK)
        at = pl.ds(start, ROW_BLOCK)
        score_block(final_chunk, False)(block, carry)
        top = jnp.max(peak[block], axis=1, keepdims=True)
        total = jnp.zeros((stacked, LANES), jnp.float32)
        summed = jnp.zeros((stacked, LANES), jnp.float32)
        for c in range(chunks):
            powers = jnp.exp(score[block, :, c * KEY_CHUNK : (c + 1) * KEY_CHUNK] - top)
            for k in range(slices):
                total = total + powers[:, k * LANES : (k + 1) * LANES]
            summed = summed + matmul(powers.astype(jnp.bfloat16), chunk_rows(c))
        result = summed / jnp.sum(total, axis=1, keepdims=True)
        low = lax.broadcasted_iota(jnp.int32, (ROW_BLOCK, LANES), 1) < HEAD_SIZE
        for pair in range(heads // 2):
            even = result[2 * pair * ROW_BLOCK : (2 * pair + 1) * ROW_BLOCK, :]
            odd = result[(2 * pair + 1) * ROW_BLOCK : (2 * pair + 2) * ROW_BLOCK, :]
            both = jnp.where(low, pltpu.roll(even, HEAD_SIZE, 1), odd)
            att[0, at, pair * LANES : (pair + 1) * LANES] = both.astype(jnp.bfloat16)
        for d in range(1, yn):
            att_copy(block, d).start()
        return carry

    lax.fori_loop(0, blocks, attend, 0)

    owner = jnp.int32(0)
    turn = jnp.int32(0)
    for r in range(zn):
        here = slots[r] == me
        owner = jnp.where(here, r, owner)
        turn = jnp.where(here, offsets[r], turn)
    for copy in entry_copies:
        copy.wait_recv()
    local[3].wait()
    entry = ents[lax.rem(me - owner + zn, zn)]
    target = lax.broadcasted_iota(jnp.int32, (KEY_CHUNK, rows), 1)
    for c in range(old_chunks):
        at = pl.ds(c * KEY_CHUNK, KEY_CHUNK)
        index = (lax.broadcasted_iota(jnp.int32, (KEY_CHUNK, rows), 0) + (c * KEY_CHUNK - turn)) & (
            WINDOW_LENGTH - 1
        )
        chosen = jnp.where(index == target, 1.0, 0.0).astype(jnp.bfloat16)
        written = matmul(chosen, entry)
        kept = old[at, :].astype(jnp.float32)
        new_cache[0, 0, at, :] = jnp.where(index[:, :LANES] < rows, written, kept).astype(jnp.bfloat16)

    for copy in w_copies:
        copy.wait_recv()
    local[5].wait()
    local[6].wait()
    part_copies = []
    for block in range(blocks):
        at = pl.ds(block * ROW_BLOCK, ROW_BLOCK)
        for d in range(1, yn):
            att_copy(block, d).wait_recv()
        pieces = [att[d, at, :] for d in range(yn)]
        other = matmul(pieces[0], wbuf[0, 1])
        for d in range(1, yn):
            other = other + matmul(pieces[d], wbuf[d, 1])
        psend[at, :] = other
        part_copies.append(
            remote(psend.at[at], precv.at[at], p_send.at[block], p_recv.at[block], sibling)
        )
        part_copies[-1].start()
        own = matmul(pieces[0], wbuf[0, 0])
        for d in range(1, yn):
            own = own + matmul(pieces[d], wbuf[d, 0])
        mine[at, :] = own
    for block in range(blocks):
        at = pl.ds(block * ROW_BLOCK, ROW_BLOCK)
        part_copies[block].wait_recv()
        mixed[at, :] = (mine[at, :] + precv[at, :]).astype(jnp.bfloat16)

    for e in range(zn):
        forward(e).wait_send()
    for copy in tok_copies + spread_copies + w_copies + gather_copies + entry_copies + part_copies:
        copy.wait_send()
    for block in range(blocks):
        for d in range(1, yn):
            att_copy(block, d).wait_send()


def per_device(
    tokens, query_weight, key_value_weight, output_weight, cache, lengths, offsets, slots
):
    zn = lax.axis_size("dp")
    yn = lax.axis_size("ty")
    rows, half_width = tokens.shape
    width = 2 * half_width
    query_cols = query_weight.shape[2]
    heads = query_cols // HEAD_SIZE
    cols = width // (2 * yn)
    piece = WINDOW_LENGTH // (2 * zn)
    blocks = rows // ROW_BLOCK

    bf16 = jnp.bfloat16
    f32 = jnp.float32
    dma = pltpu.SemaphoreType.DMA
    hbm = pl.BlockSpec(memory_space=pltpu.HBM)
    vmem = pl.BlockSpec(memory_space=pltpu.VMEM)
    flops = 2 * rows * (width * (query_cols + 2 * HEAD_SIZE + width // yn) + 4 * query_cols * (WINDOW_LENGTH + rows))
    return pl.pallas_call(
        functools.partial(kernel, zn, yn),
        out_shape=(
            jax.ShapeDtypeStruct((rows, cols), bf16),
            jax.ShapeDtypeStruct(cache.shape, bf16),
        ),
        in_specs=[hbm] * 8,
        out_specs=(vmem, vmem),
        scratch_shapes=[
            pltpu.SMEM(lengths.shape, jnp.int32),
            pltpu.SMEM(offsets.shape, jnp.int32),
            pltpu.SMEM(slots.shape, jnp.int32),
            pltpu.VMEM((rows, LANES), f32),
            pltpu.VMEM((rows, LANES), f32),
            pltpu.VMEM((2, rows, half_width), bf16),
            pltpu.VMEM((width, query_cols), bf16),
            pltpu.VMEM((width, 2 * HEAD_SIZE), bf16),
            pltpu.VMEM((WINDOW_LENGTH, 2 * HEAD_SIZE), bf16),
            pltpu.VMEM((yn, 2, query_cols, cols), bf16),
            pltpu.VMEM((zn, piece, 2 * HEAD_SIZE), bf16),
            pltpu.VMEM((zn, piece, 2 * HEAD_SIZE), bf16),
            pltpu.VMEM((WINDOW_LENGTH + rows, 2 * HEAD_SIZE), bf16),
            pltpu.VMEM((zn, rows, 2 * HEAD_SIZE), bf16),
            pltpu.VMEM((heads, rows, LANES), bf16),
            pltpu.VMEM((yn, rows, query_cols), bf16),
            pltpu.VMEM((blocks, heads * ROW_BLOCK, WINDOW_LENGTH + rows), f32),
            pltpu.VMEM((blocks, heads * ROW_BLOCK, LANES), f32),
            pltpu.VMEM((rows, cols), f32),
            pltpu.VMEM((rows, cols), f32),
            pltpu.VMEM((rows, cols), f32),
            dma((10,)),
            dma((rows // PROJECT_ROWS,)),
            dma((rows // PROJECT_ROWS,)),
            dma((yn, 2)),
            dma((yn, 2)),
            dma((zn,)),
            dma((zn,)),
            dma((zn,)),
            dma((zn,)),
            dma((zn,)),
            dma((zn,)),
            dma((zn,)),
            dma((zn,)),
            dma((blocks, yn)),
            dma((blocks, yn)),
            dma((blocks,)),
            dma((blocks,)),
        ],
        compiler_params=pltpu.CompilerParams(
            collective_id=0, has_side_effects=True, vmem_limit_bytes=56 * 1024 * 1024
        ),
        cost_estimate=pl.CostEstimate(flops=flops, bytes_accessed=6 << 20, transcendentals=0),
    )(
        tokens,
        query_weight.reshape(width, query_cols),
        key_value_weight.reshape(width, 2 * HEAD_SIZE),
        output_weight,
        cache,
        lengths,
        offsets,
        slots,
    )


def solution(mesh):
    return jax.shard_map(
        per_device,
        mesh=mesh,
        in_specs=(
            P("dp", "tx"),
            P(None, "ty", "tx"),
            P(None, "ty", None),
            P("ty", "tx", None),
            P("dp", "ty", None, None),
            P(),
            P(),
            P(),
        ),
        out_specs=(P("dp", ("tx", "ty")), P("dp", "ty", None, None)),
        check_vma=False,
    )
```
